32 devices in a mesh: dp: 16 (over z, y, core), fsdp: 2 (over x).
Axes of the slice: x: 2, y: 2, z: 4, core: 2. Of those that a mesh axis runs over, the one named last changes fastest.
Arguments:
- tokens: bfloat16 [64, 656, 768], P(('dp', 'fsdp')), may hold values from -6 to 6
- groups: int32 [64, 656], P(('dp', 'fsdp')), may hold values from 0 to 4, as said below
- step_valid: int32 [64, 2], P(('dp', 'fsdp')), may hold values 0 or 1
- query_weight: bfloat16 [768, 768], P('dp', 'fsdp'), may hold values from -0.21875 to 0.21875
- key_weight: bfloat16 [768, 768], P('dp', 'fsdp'), may hold values from -0.21875 to 0.21875
- value_weight: bfloat16 [768, 768], P('dp', 'fsdp'), may hold values from -0.21875 to 0.21875
- output_weight: bfloat16 [768, 768], P('dp', 'fsdp'), may hold values from -1.75 to 1.75
- up_weight: bfloat16 [768, 3072], P('dp', 'fsdp'), may hold values from -0.21875 to 0.21875
- down_weight: bfloat16 [3072, 768], P('dp', 'fsdp'), may hold values from -0.109375 to 0.109375
- vectors: bfloat16 [8, 768], P('fsdp', 'dp')
- up_bias: bfloat16 [3072], P(('dp', 'fsdp')), may hold values from -3 to 3
- cotangent: bfloat16 [64, 656, 768], P(('dp', 'fsdp')), may hold values from -6 to 6
Outputs:
- result: bfloat16 [64, 656, 768], P(('dp', 'fsdp'))
- grad_tokens: bfloat16 [64, 656, 768], P(('dp', 'fsdp'))
- grad_query: float32 [768, 768], P('dp', 'fsdp')
- grad_key: float32 [768, 768], P('dp', 'fsdp')
- grad_value: float32 [768, 768], P('dp', 'fsdp')
- grad_output: float32 [768, 768], P('dp', 'fsdp')
- grad_up: float32 [768, 3072], P('dp', 'fsdp')
- grad_down: float32 [3072, 768], P('dp', 'fsdp')
- grad_vectors: float32 [8, 768], P('fsdp', 'dp')
- grad_up_bias: float32 [3072], P(('dp', 'fsdp'))
The draws below stay inside these ranges and needn't reach their ends.
Inputs may be any that keep to these rules, and one draw needn't show every extreme that they name: In each item 12 positions hold group 0, and for each timestep 256 + 64 positions hold group 2t + 1 and 2 positions group 2t + 2; the positions of the groups are in any order.
All inputs are finite; a program needn't handle non-finite values. No bound on the sum of `step_valid` on one device may be relied on, other than what follows from the above.
Results may differ from the reference program's by a relative error of at most 0.011.
Values may be sent and summed in bfloat16 or wider, within the bound.
A program may use at most 192 MiB of HBM per device.

```python
import jax
import jax.numpy as jnp
from jax import lax

D = 768
HEADS = 12
HD = 64
FF = 3072
TASK = 12
PRIMARY = 256
WRIST = 64
READOUT = 2
STEPS = 2
SEQ = 656
ITEMS = 64


def draw_groups(key, part):
    key = jax.random.fold_in(key, 7)
    per_step = PRIMARY + WRIST + READOUT
    position = jnp.arange(SEQ, dtype=jnp.int32)
    offset = jnp.maximum(position - TASK, 0)
    within = offset % per_step
    layout = jnp.where(position < TASK, 0, 1 + 2 * (offset // per_step) + (within >= PRIMARY + WRIST).astype(jnp.int32))
    item_keys = jax.random.split(key, ITEMS)

    def shuffle(item_key):
        return jax.random.permutation(item_key, layout)
    return jax.vmap(shuffle)(item_keys).astype(jnp.int32)


def draw_vectors(key, part):
    key = jax.random.fold_in(key, 11)
    spread_draw = jax.random.uniform(key, (8, D), jnp.float32, -1.0, 1.0)
    row_index = jnp.arange(8)[:, None]
    gain_rows = (row_index == 0) | (row_index == 5)
    return jnp.where(gain_rows, 1.0 + 0.4 * spread_draw, 0.5 * spread_draw).astype(jnp.bfloat16)


def with_ends(values, stream_key, least, largest):
    longest = values.shape.index(max(values.shape))
    spots = []
    for shift in (0, 1):
        where = [jax.random.randint(jax.random.fold_in(stream_key, axis), (), 0, length) for axis, length in enumerate(values.shape)]
        where[longest] = (where[longest] + shift) % values.shape[longest]
        spots.append(tuple(where))
    return values.at[spots[0]].set(least).at[spots[1]].set(largest)


def strengthened(result, stream_key, source, target, shards_of, factor):
    def block_of(axis_at):
        return (jnp.arange(result.shape[axis_at]) // (result.shape[axis_at] // shards_of)).reshape((-1,) + (1,) * (result.ndim - 1 - axis_at))

    near = jax.random.permutation(stream_key, shards_of)[block_of(target)]
    second = (block_of(target) + shards_of // 2) % shards_of
    return jnp.where((block_of(source) == near) | (block_of(source) == second), factor * result, result)


def steps_of(own_key, shape, cuts, least, top_value):
    def one(dim, shards_of):
        heights = jax.random.uniform(jax.random.fold_in(jax.random.fold_in(own_key, 6), dim), (shards_of,), jnp.float32, least / len(cuts), top_value / len(cuts))
        return jnp.repeat(jnp.exp(heights), shape[dim] // shards_of).reshape((-1,) + (1,) * (len(shape) - dim - 1))

    factor_of = one(*cuts[0])
    for cut in cuts[1:]:
        factor_of = factor_of * one(*cut)
    return factor_of


def gaussian(key, extent, deviation, limit, cuts=(), kind=jnp.bfloat16):
    level = steps_of(key, extent, cuts, -0.22, 0.18) if cuts else 1.0
    entries = jax.random.normal(key, extent, jnp.float32) * deviation * level
    return jnp.minimum(jnp.maximum(entries, -limit), limit).astype(kind)


def gaussian_with(stream_key, shape, scale, bound, cuts, heavy, kind=jnp.bfloat16):
    values = scale * jax.random.normal(stream_key, shape, jnp.float32)
    if cuts:
        values = values * steps_of(stream_key, shape, cuts, -0.22, 0.18)
    return jnp.clip(strengthened(values, jax.random.fold_in(stream_key, 3), *heavy), -bound, bound).astype(kind)


def setup_inputs(seed: int = 0) -> dict:
    keys = jax.random.split(jax.random.key(seed), 13)
    return {
        "tokens": gaussian(keys[0], (ITEMS, SEQ, D), 1.0, 6.0, ((0, 32),)),
        "groups": draw_groups(jax.random.fold_in(keys[12], 71), 0),
        "step_valid": with_ends((jax.random.randint(keys[2], (ITEMS, STEPS), 0, 4) < 3).astype(jnp.int32), jax.random.fold_in(keys[2], 1), 0, 1),
        "query_weight": gaussian(keys[3], (D, D), D ** -0.5, 0.21875, ((0, 16), (1, 2))),
        "key_weight": gaussian(keys[4], (D, D), D ** -0.5, 0.21875, ((0, 16), (1, 2))),
        "value_weight": gaussian(keys[5], (D, D), D ** -0.5, 0.21875, ((0, 16), (1, 2))),
        "output_weight": gaussian(keys[6], (D, D), (D // 64) ** -0.5, 1.75, ((0, 16), (1, 2))),
        "up_weight": gaussian(keys[7], (D, FF), D ** -0.5, 0.21875, ((0, 16), (1, 2))),
        "down_weight": gaussian(keys[8], (FF, D), FF ** -0.5, 0.109375, ((0, 16), (1, 2))),
        "vectors": draw_vectors(jax.random.fold_in(keys[12], 71), 0),
        "up_bias": gaussian(keys[10], (FF,), 0.5, 3.0, ((0, 32),)),
        "cotangent": gaussian_with(keys[11], (ITEMS, SEQ, D), 1.0, 6.0, ((0, 32),), (0, 2, 32, 2.75)),
    }


@jax.custom_vjp
def low(v):
    return lax.optimization_barrier(v.astype(jnp.bfloat16)).astype(jnp.float32)

@jax.custom_vjp
def low_back(v):
    return v

def low_keep(v):
    return (low(v), None)

def low_pass(kept, grad):
    return (grad,)

def back_keep(v):
    return (v, None)

def back_low(kept, grad):
    return (low(grad),)
low.defvjp(low_keep, low_pass)
low_back.defvjp(back_keep, back_low)
eps = 1e-06
masked_score = -1e+30

def product(left, right):
    return jnp.dot(left, right, precision=lax.Precision.HIGHEST, preferred_element_type=jnp.float32)

def layer_norm(rows_in, gain, shift):
    center = rows_in - lax.optimization_barrier(jnp.mean(rows_in, axis=-1, keepdims=True))
    spread_sq = lax.optimization_barrier(jnp.mean(center * center, axis=-1, keepdims=True))
    return center * lax.rsqrt(spread_sq + eps) * gain + shift

def visible(groups, step_valid):
    query_group = groups[:, None]
    key_group = groups[None, :]
    linked = (key_group == 0) | (key_group == query_group) | (key_group % 2 == 1) & (key_group < query_group)
    step_ids = jnp.arange(step_valid.shape[0], dtype=jnp.int32)
    owned = ((groups[:, None] - 1) // 2 == step_ids[None, :]) & (step_valid[None, :] == 1)
    alive_keys = (groups == 0) | jnp.any(owned, axis=1)
    return linked & alive_keys[None, :]

def heads_of(block):
    return block.reshape(block.shape[0], HEADS, HD).transpose(1, 0, 2)

def item_forward(inputs, groups, step_valid, query_weight, key_weight, value_weight, output_weight, up_weight, down_weight, vectors, up_bias):
    length = inputs.shape[0]
    normed = low(layer_norm(inputs, vectors[0], vectors[1]))
    queries = low_back(low(product(normed, query_weight) + vectors[2]))
    key_rows = low_back(low(product(normed, key_weight)))
    values = low_back(low(product(normed, value_weight) + vectors[3]))
    raw = jnp.einsum('hqd,hkd->hqk', heads_of(queries), heads_of(key_rows), precision=lax.Precision.HIGHEST)
    scores = low_back(raw * HD ** (-0.5))
    scores = jnp.where(visible(groups, step_valid)[None], scores, masked_score)
    probs = jax.nn.softmax(scores, axis=-1)
    mixture = jnp.einsum('hqk,hkd->hqd', low(probs), heads_of(values), precision=lax.Precision.HIGHEST)
    mixture = low_back(low(mixture.transpose(1, 0, 2).reshape(length, HEADS * HD)))
    branch = low_back(product(mixture, output_weight) + vectors[4])
    middle = inputs + branch
    second = low(layer_norm(middle, vectors[5], vectors[6]))
    pre = low_back(product(second, up_weight) + up_bias)
    hidden = low(jax.nn.gelu(pre))
    return middle + product(hidden, down_weight) + vectors[7]

def reference(tokens, groups, step_valid, query_weight, key_weight, value_weight, output_weight, up_weight, down_weight, vectors, up_bias, cotangent):
    weights = tuple((item.astype(jnp.float32) for item in (query_weight, key_weight, value_weight, output_weight, up_weight, down_weight, vectors, up_bias)))
    inputs = tokens.astype(jnp.float32)

    def forward(all_inputs, all_weights):

        def one_item(packed):
            rows_in, item_groups, item_valid = packed
            return item_forward(rows_in, item_groups, item_valid, *all_weights)
        return lax.map(jax.checkpoint(one_item), (all_inputs, groups, step_valid))
    output, pull = jax.vjp(forward, inputs, weights)
    grad_inputs, grad_weights = pull(cotangent.astype(jnp.float32))
    return (output.astype(jnp.bfloat16), grad_inputs.astype(jnp.bfloat16), grad_weights[0], grad_weights[1], grad_weights[2], grad_weights[3], grad_weights[4], grad_weights[5], grad_weights[6], grad_weights[7])
```

```python
import functools

import jax
import jax.numpy as jnp
from jax import lax
from jax.experimental import pallas as pl
from jax.experimental.pallas import tpu as pltpu
from jax.sharding import PartitionSpec as P

bf = jnp.bfloat16
f32 = jnp.float32
NN = (((1,), (0,)), ((), ()))
NT = (((1,), (1,)), ((), ()))
TN = (((0,), (0,)), ((), ()))
HD = 64
EPS = 1e-6
MESH = pl.DeviceIdType.MESH
VMEM = pltpu.VMEM
DMA = pltpu.SemaphoreType.DMA


def dg(a, b, dims):
    return lax.dot_general(a, b, dims, preferred_element_type=f32)


def mat(ref):
    block = ref[...]
    return block.reshape(-1, block.shape[-1])


def normalized(x):
    center = x - jnp.mean(x, axis=-1, keepdims=True)
    r = lax.rsqrt(jnp.mean(center * center, axis=-1, keepdims=True) + EPS)
    return center * r, r


def fold8(x):
    return jnp.sum(x.reshape(-1, 8, x.shape[-1]), axis=0)


def each_block(rows, body, sums=None, size=32, together=5):
    step = size * together
    whole = rows // step

    def several(blocks):
        parts = [body(at, n) for at, n in blocks]
        for i in range(len(parts[0] or ())):
            sums[i] += sum(part[i] for part in parts)

    def one(i, c):
        several([(pl.ds(pl.multiple_of(i * step + k * size, 16), size), size) for k in range(together)])
        return c

    lax.fori_loop(0, whole, one, 0)
    if whole * step < rows:
        several([(pl.ds(at, min(size, rows - at)), min(size, rows - at)) for at in range(whole * step, rows, size)])


class Core:
    def __init__(self, rows, length, width, chunks, refs):
        self.rows, self.length, self.width, self.chunks = rows, length, width, chunks
        self.items = rows // length
        self.pairs = width // 128
        self.steps = self.pairs // 2
        self.__dict__.update(refs)

    def blocks(self):
        half = (self.length // 2 + 15) // 16 * 16
        return ((0, half), (half, self.length - half))

    def norm_one(self):
        def block(at, size):
            self.res[at, :] = normalized(self.x[at, :].astype(f32))[0]

        each_block(self.rows, block)

    def norm_one_scaled(self):
        gain, shift = self.vec[0:1, :], self.vec[1:2, :]

        def block(at, size):
            self.normed[at, :] = (self.res[at, :] * gain + shift).astype(bf)

        each_block(self.rows, block)

    def project(self, s):
        step = self.steps

        def three(p):
            at = slice(128 * p, 128 * p + 128)
            return [self.vec[2:3, at], jnp.zeros((1, 128), f32), self.vec[3:4, at]]

        bias = jnp.concatenate(three(s) + three(s + step), axis=1)
        lane = lax.broadcasted_iota(jnp.int32, (1, self.width), 1) % 384
        scale = jnp.where(lane < 128, HD**-0.5, 1.0).astype(f32)
        out = (dg(self.normed[...], mat(self.wqkv.at[s]), NN) + bias) * scale
        self.qkv[s % 2] = out.astype(bf)

    def place(self, s, u):
        item, half = u // 2, u % 2
        rows = pl.ds(pl.multiple_of(item * self.length, 16), self.length)
        cols = [pl.ds(pl.multiple_of(half * 384 + 128 * w, 128), 128) for w in range(3)]
        wide = pl.ds(pl.multiple_of((s + half * self.steps) * 128, 128), 128)
        return rows, cols, wide

    def low(self):
        return lax.broadcasted_iota(jnp.int32, (self.length, 128), 1) < HD

    def attend(self, s, u):
        n = 2 * self.items
        rows, cols, wide = self.place(s, u)
        q, k, v = [self.qkv[s % 2, rows, at] for at in cols]
        g, b = self.onehot[rows, :], self.bias[rows, :]
        low = self.low()
        t = s * n + u
        outs = []
        for h in (0, 1):

            @pl.when(t >= 1)
            def _():
                self.keep_probs(t - 1, h).wait()

            mine = low if h == 0 else ~low
            qa, ka = jnp.where(mine, q, g), jnp.where(mine, k, b)
            va = jnp.where(mine, v, jnp.ones_like(v))
            parts = []
            for at, size in self.blocks():
                scores = dg(qa[at : at + size], ka, NT)
                e = jnp.exp(scores - jnp.max(scores, axis=1, keepdims=True)).astype(bf)
                self.ebuf[h, at : at + size, :] = e
                parts.append(dg(e, va, NN))
            self.keep_probs(t, h).start()
            outs.append(jnp.concatenate(parts, axis=0))
        total = pltpu.roll(jnp.where(low, outs[1], outs[0]), HD, 1)
        inv = 1.0 / total
        self.linv[rows, wide] = inv.astype(bf)
        self.mix[rows, wide] = (jnp.where(low, outs[0], outs[1]) * inv).astype(bf)

    def keep_probs(self, t, h):
        return pltpu.make_async_copy(self.ebuf.at[h], self.e_hbm.at[2 * t + h], self.e_sem.at[h])

    def attend_end(self):
        for h in (0, 1):
            self.keep_probs(2 * self.items * self.steps - 1, h).wait()

    def output(self):
        self.res[...] = dg(self.mix[...], mat(self.wo), NN)
        shift0, gain, shift = self.vec[4:5, :], self.vec[5:6, :], self.vec[6:7, :]

        def block(at, size):
            middle = self.res[at, :] + self.x[at, :].astype(f32) + shift0
            self.res[at, :] = middle
            n, r = normalized(middle)
            self.n2[at, :] = n.astype(bf)
            self.r2[at, :] = jnp.broadcast_to(r, (size, 128))
            self.second[at, :] = (n * gain + shift).astype(bf)

        each_block(self.rows, block)
        self.gsec[...] = jnp.zeros_like(self.gsec)

    def feed(self, j):
        z, y = lax.div(j, 2), lax.rem(j, 2)
        first, other = self.down.at[z, y], self.down.at[2 + z, 1 - y]
        up = mat(self.up.at[j])
        down = jnp.concatenate([mat(first), mat(other)], axis=0)
        bias = self.vec[pl.ds(8 + j, 1), :]
        c0, c1 = 0.7978845608028654, 0.7978845608028654 * 0.044715

        def item(i, c):
            for at, size in self.blocks():
                rows = pl.ds(pl.multiple_of(i * self.length + at, 16), size)
                u = dg(self.second[rows, :], up, NN) + bias
                gh = dg(self.cot[rows, :], down, NT)
                u2 = u * u
                s = 0.5 + 0.5 * jnp.tanh(u * (c0 + c1 * u2))
                hid = u * s
                slope = s + (hid * (1.0 - s)) * (2 * c0 + (6 * c1) * u2)
                gp = gh * slope
                hid, gp = hid.astype(bf), gp.astype(bf)
                self.hid[rows, :] = hid
                self.gp[rows, :] = gp
                self.sums8[1] += fold8(gp.astype(f32))
                self.res[rows, :] += dg(hid, down, NN)
                self.gsec[rows, :] += dg(gp, up, NT)
            return c

        self.sums8[1] = jnp.zeros_like(self.sums8[1])
        lax.fori_loop(0, self.items, item, 0)
        self.small[pl.ds(8 + j, 1), :] = jnp.sum(self.sums8[1], axis=0, keepdims=True)
        gup = dg(self.second[...], self.gp[...], TN).astype(bf)
        self.up[j] = gup.reshape(self.up.shape[1:])
        gdown = dg(self.hid[...], self.cot[...], TN).astype(bf)
        half = gdown.shape[0] // 2
        first[...] = gdown[:half].reshape(first.shape)
        other[...] = gdown[half:].reshape(other.shape)

    def norm_two_back(self):
        gain, last = self.vec[5:6, :], self.vec[7:8, :]
        self.sums8[...] = jnp.zeros_like(self.sums8)

        def block(at, size):
            self.result[at, :] = (self.res[at, :] + last).astype(bf)
            gs, n, r = self.gsec[at, :], self.n2[at, :].astype(f32), self.r2[at, 0:1]
            ct = self.cot[at, :].astype(f32)
            e = gs * gain
            gm = ct + r * (e - jnp.mean(e, axis=-1, keepdims=True) - n * jnp.mean(e * n, axis=-1, keepdims=True))
            gb = gm.astype(bf)
            self.gsec[at, :] = gm
            self.gp[at, :] = gb
            return fold8(gb.astype(f32)), fold8(gs * n), fold8(gs), fold8(ct)

        each_block(self.rows, block, self.sums8)
        for i in range(4):
            self.small[4 + i : 5 + i, :] = jnp.sum(self.sums8[i], axis=0, keepdims=True)

    def output_back(self):
        self.hid[...] = dg(self.gp[...], mat(self.wo), NT).astype(bf)
        self.wo[...] = dg(self.mix[...], self.gp[...], TN).astype(bf).reshape(self.wo.shape)

    def fetch_probs(self, t, h):
        return pltpu.make_async_copy(self.e_hbm.at[2 * t + h], self.ebuf.at[h], self.e_sem.at[h])

    def attend_back(self, s, u):
        n = 2 * self.items
        rows, cols, wide = self.place(s, u)
        t = s * n + u
        after = t + 1 - lax.div(u + 1, n) * 2 * n
        q, k, v = [self.qkv[s % 2, rows, at] for at in cols]
        low = self.low()
        lane = lax.broadcasted_iota(jnp.int32, (self.length, 128), 1) % HD
        across = lax.broadcasted_iota(jnp.int32, (128, 128), 0) // HD != lax.broadcasted_iota(jnp.int32, (128, 128), 1) // HD
        across = jnp.where(across, 1.0, 0.0).astype(bf)
        go = self.hid[rows, wide].astype(f32) * self.linv[rows, wide].astype(f32)
        gob = go.astype(bf)
        inner = dg((go * self.mix[rows, wide].astype(f32)).astype(bf), across, NN)
        high = inner.astype(bf)
        rest = (inner - high.astype(f32)).astype(bf)
        minus = jnp.where(lane == 0, -high, jnp.where(lane == 1, -rest, jnp.zeros_like(high)))
        qt, kt, gt = q.T, k.T, gob.T
        dq, dk, dv = [], [], []
        for h in (0, 1):
            mine = low if h == 0 else ~low
            ga, va = jnp.where(mine, gob, minus), jnp.where(mine, v, jnp.ones_like(v))
            at_h = slice(HD * h, HD * h + HD)
            self.fetch_probs(t, h).wait()
            for at, size in self.blocks():
                gprobs = dg(ga[at : at + size], va, NT)
                self.dsbuf[at : at + size, :] = (self.ebuf[h, at : at + size, :].astype(f32) * gprobs).astype(bf)
            ds, e = self.dsbuf[...], self.ebuf[h]
            dq.append(dg(kt[at_h], ds, NT))
            dk.append(dg(qt[at_h], ds, NN))
            dv.append(dg(gt[at_h], e, NN))

            @pl.when(after >= 0)
            def _():
                self.fetch_probs(after, h).start()

        for at, part, scale in zip(cols, (dq, dk, dv), (HD**-0.5, 1.0, 1.0)):
            whole = (jnp.concatenate(part, axis=0) * scale).T
            self.gp[rows, at] = whole.astype(bf)

    def normed_back(self, s):
        part = dg(self.gp[...], mat(self.wqkv.at[s]), NT)
        if s == self.steps - 1:
            self.res[...] = part
        else:
            self.res[...] += part

    def project_back(self, s):
        self.wqkv[s] = dg(self.normed[...], self.gp[...], TN).astype(bf).reshape(self.wqkv.shape[1:])
        self.sums8[0] = jnp.zeros_like(self.sums8[0])
        each_block(self.rows, lambda at, size: (fold8(self.gp[at, :].astype(f32)),), self.sums8)
        total = jnp.sum(self.sums8[0], axis=0, keepdims=True)
        for half in (0, 1):
            p = s + half * self.steps
            for row, w in ((2, 0), (3, 2)):
                at = half * 384 + 128 * w
                self.small[row : row + 1, 128 * p : 128 * p + 128] = total[:, at : at + 128]

    def norm_one_back(self):
        gain = self.vec[0:1, :]
        self.sums8[...] = jnp.zeros_like(self.sums8)

        def block(at, size):
            n, r = normalized(self.x_back[at, :].astype(f32))
            gn = self.res[at, :]
            e = gn * gain
            gt = self.gsec[at, :] + r * (e - jnp.mean(e, axis=-1, keepdims=True) - n * jnp.mean(e * n, axis=-1, keepdims=True))
            self.gtok[at, :] = gt.astype(bf)
            return fold8(gn * n), fold8(gn)

        each_block(self.rows, block, self.sums8)
        for i in range(2):
            self.small[i : i + 1, :] = jnp.sum(self.sums8[i], axis=0, keepdims=True)


class Links:
    def __init__(self, refs, views, sources, sums):
        dp = lax.axis_index("dp")
        self.f = lax.axis_index("fsdp")
        self.z, self.y, self.c = dp // 4, (dp // 2) % 2, dp % 2
        self.views, self.sources, self.sums = views, sources, sums
        self.__dict__.update(refs)

    def at(self, z=None, y=None, c=None, f=None):
        z = self.z if z is None else z
        y = self.y if y is None else y
        c = self.c if c is None else c
        f = self.f if f is None else f
        return (z * 4 + y * 2 + c, f)

    def along_z(self, d):
        return self.at(z=(self.z + d) % 4)

    def across(self, axis):
        return dict(x=self.at(f=1 - self.f), y=self.at(y=1 - self.y), c=self.at(c=1 - self.c))[axis]

    def greet(self):
        barrier = pltpu.get_barrier_semaphore()
        for peer in [self.along_z(d) for d in (1, 2, 3)] + [self.across(axis) for axis in "xyc"]:
            pl.semaphore_signal(barrier, inc=1, device_id=peer, device_id_type=MESH)
        pl.semaphore_wait(barrier, 6)

    def half(self, f, width):
        return pl.ds(pl.multiple_of(f * (width // 2), 128), width // 2)

    def send(self, src, dst, sem, peer):
        return pltpu.make_async_remote_copy(
            src_ref=src,
            dst_ref=dst,
            send_sem=self.send_sem.at[sem],
            recv_sem=self.recv_sem.at[sem],
            device_id=peer,
            device_id_type=MESH,
        )

    def own_copies(self, g):
        view = self.views[g]
        first = self.f * (view.shape[-1] // 2)
        copies = []
        for i, (piece, at, size) in enumerate(self.sources[g]):
            spot = view.at[self.z, self.y, self.c, :, pl.ds(pl.multiple_of(first + at, 128), size)]
            copies.append(pltpu.make_async_copy(piece, spot, self.own_sem.at[3 * g + i]))
        return copies

    def own(self, g):
        for copy in self.own_copies(g):
            copy.start()

    def gather_copies(self, g, stage):
        view = self.views[g]
        mine = self.half(self.f, view.shape[-1])
        first, second = "xy" if g % 2 == 0 else "yx"
        base = 6 * g
        if stage == 0:
            spot = view.at[self.z, self.y, self.c, :, mine]
            return [self.send(spot, spot, base + d - 1, self.along_z(d)) for d in (1, 2, 3)]
        if stage == 1:
            part = view.at[:, self.y, self.c, :, mine]
            return [self.send(part, part, base + 3, self.across(first))]
        if stage == 2:
            part = view.at[:, self.y, self.c] if first == "x" else view.at[:, :, self.c, :, mine]
            return [self.send(part, part, base + 4, self.across(second))]
        part = view.at[:, :, self.c]
        return [self.send(part, part, base + 5, self.across("c"))]

    def gather(self, g, stage):
        for copy in self.own_copies(g) if stage == 0 else self.gather_copies(g, stage - 1):
            copy.wait()
        if stage < 4:
            for copy in self.gather_copies(g, stage):
                copy.start()

    def scatter_copies(self, p, stage):
        view = self.views[SUMMED[p]]
        width = view.shape[-1]
        mine, other = self.half(self.f, width), self.half(1 - self.f, width)
        first, second = "xy" if p % 2 == 0 else "yx"
        base = 6 * (len(self.views) + p)
        if stage == 0:
            return [self.send(view.at[:, :, 1 - self.c], self.got_c.at[p % self.got_c.shape[0]], base, self.across("c"))]
        if stage == 1 and first == "x":
            return [self.send(view.at[:, :, self.c, :, other], self.got_x.at[p // 2], base + 1, self.across("x"))]
        if stage == 1:
            return [self.send(view.at[:, 1 - self.y, self.c], self.got_y.at[p // 2], base + 1, self.across("y"))]
        if stage == 2:
            part = view.at[:, 1 - self.y, self.c, :, mine] if second == "y" else view.at[:, self.y, self.c, :, other]
            return [self.send(part, self.got_2.at[p], base + 2, self.across(second))]
        copies = []
        for d in (1, 2, 3):
            part = view.at[(self.z + d) % 4, self.y, self.c, :, mine]
            copies.append(self.send(part, self.got_z.at[p, d - 1], base + 2 + d, self.along_z(d)))
        return copies

    def scatter(self, p, stage):
        view = self.views[SUMMED[p]]
        mine = self.half(self.f, view.shape[-1])
        slots = self.got_c.shape[0]
        if stage > 0:
            for copy in self.scatter_copies(p, stage - 1):
                copy.wait()
        if stage == 1:
            for z in range(4):
                for y in range(2):
                    view[z, y, self.c] += self.got_c[p % slots, z, y]
            if p + slots < len(self.views):
                pl.semaphore_signal(self.free_sem, inc=1, device_id=self.across("c"), device_id_type=MESH)
        if stage == 2 and p % 2 == 0:
            for z in range(4):
                for y in range(2):
                    view[z, y, self.c, :, mine] += self.got_x[p // 2, z, y]
        if stage == 2 and p % 2 == 1:
            for z in range(4):
                view[z, self.y, self.c] += self.got_y[p // 2, z]
        if stage == 3:
            for z in range(4):
                view[z, self.y, self.c, :, mine] += self.got_2[p, z]
        if stage == 4:
            total = view[self.z, self.y, self.c, :, mine].astype(f32)
            for d in range(3):
                total += self.got_z[p, d].astype(f32)
            self.sums[SUMMED[p]] = total
            return
        if stage == 0 and p >= slots:
            pl.semaphore_wait(self.free_sem, 1)
        for copy in self.scatter_copies(p, stage):
            copy.start()

    def small_copies(self, which, stage):
        mine, got = (self.vec, self.small)[which], self.got_v.at[which]
        base = 12 * len(self.views) + 6 * which
        if stage == 0:
            return [self.send(mine, got.at[d - 1], base + d - 1, self.along_z(d)) for d in (1, 2, 3)]
        return [self.send(mine, got.at[2 + stage], base + 2 + stage, self.across("xyc"[stage - 1]))]

    def small_sum(self, which, stage):
        mine = (self.vec, self.small)[which]
        if stage > 0:
            for copy in self.small_copies(which, stage - 1):
                copy.wait()
            got = self.got_v
            mine[...] += sum(got[which, i] for i in range(3)) if stage == 1 else got[which, 1 + stage]
        if stage < 4:
            for copy in self.small_copies(which, stage):
                copy.start()


def link_scratch(groups, rows, width, slots):
    return dict(
        vec=VMEM((16, width), f32),
        got_v=VMEM((2, 6, 16, width), f32),
        got_c=VMEM((slots, 4, 2, rows, width), bf),
        got_x=VMEM((groups // 2, 4, 2, rows, width // 2), bf),
        got_y=VMEM((groups // 2, 4, rows, width), bf),
        got_2=VMEM((groups, 4, rows, width // 2), bf),
        got_z=VMEM((groups, 3, rows, width // 2), bf),
        send_sem=DMA((12 * groups + 12,)),
        recv_sem=DMA((12 * groups + 12,)),
        own_sem=DMA((3 * groups,)),
        free_sem=pltpu.SemaphoreType.REGULAR,
    )


def masks(groups, step_valid):
    rows = groups.reshape(-1, 1)
    valid = jnp.repeat(step_valid, groups.shape[1], axis=0)
    steps = step_valid.shape[1]
    lane = jnp.arange(128, dtype=jnp.int32)[None, :] % HD
    onehot = (rows == lane).astype(bf)
    linked = (rows == 0) | (rows == lane) | (rows % 2 == 1) & (rows < lane)
    alive = rows == 0
    for t in range(steps):
        alive = alive | (((rows - 1) // 2 == t) & (rows > 0) & (valid[:, t : t + 1] == 1))
    hidden = ~(linked & alive) & (lane <= 2 * steps)
    return onehot, jnp.where(hidden, -1e30, 0.0).astype(bf)


WEIGHTS = ("wqkv", "wo", "up", "down")


def local_scratch(rows, length, width, ff):
    whole = (rows, width)
    steps, cut = width // 256, width // 16
    return dict(
        wqkv=VMEM((steps, 4, 2, 2, cut, width), bf),
        wo=VMEM((4, 2, 2, cut, width), bf),
        up=VMEM((ff // width, 4, 2, 2, cut, width), bf),
        down=VMEM((4, 2, 2, ff // 16, width), bf),
        cot=VMEM(whole, bf),
        normed=VMEM(whole, bf),
        qkv=VMEM((2,) + whole, bf),
        mix=VMEM(whole, bf),
        linv=VMEM(whole, bf),
        res=VMEM(whole, f32),
        n2=VMEM(whole, bf),
        r2=VMEM((rows, 128), f32),
        second=VMEM(whole, bf),
        gsec=VMEM(whole, f32),
        hid=VMEM(whole, bf),
        gp=VMEM(whole, bf),
        ebuf=VMEM((2, length, length), bf),
        dsbuf=VMEM((length, length), bf),
        sums8=VMEM((4, 8, width), f32),
        e_sem=DMA((2,)),
        in_sem=DMA((4,)),
    )


def layer(length, core_refs, hbm, tick, links_on):
    r = core_refs
    rows, width = r["mix"].shape
    x, cot, result, gtok, qkv_hbm = [hbm[k] for k in ("x", "cot", "result", "gtok", "qkv_hbm")]
    core = Core(rows, length, width, r["up"].shape[0], dict(r, x=r["hid"], x_back=r["second"], result=r["second"], gtok=r["n2"], e_hbm=hbm["e_hbm"]))
    load_x = pltpu.make_async_copy(x, r["hid"], r["in_sem"].at[0])
    load_cot = pltpu.make_async_copy(cot, r["cot"], r["in_sem"].at[1])
    keep_qkv = pltpu.make_async_copy(r["qkv"].at[0], qkv_hbm, r["in_sem"].at[2])
    units = 2 * core.items

    def each_unit(name, work):
        def one(u, c):
            for k in range(units):
                if tick(name + str(k), True):
                    pl.when(u == k)(functools.partial(tick, name + str(k)))
            work(u)
            return c

        lax.fori_loop(0, units, one, 0)

    load_x.start()
    load_cot.start()
    r["small"][...] = jnp.zeros_like(r["small"])
    tick("start")
    load_x.wait()
    core.norm_one()
    tick("head")
    core.norm_one_scaled()
    for s in range(core.steps):
        tick(f"project{s}")
        if s == 2:
            keep_qkv.wait()
        core.project(s)
        if s == 0:
            keep_qkv.start()
        each_unit(f"attend{s}.", functools.partial(core.attend, s))
    core.attend_end()
    tick("output")
    core.output()
    load_cot.wait()

    def feed(j, c):
        for k in range(core.chunks):
            if tick(f"feed{k}", True):
                pl.when(j == k)(functools.partial(tick, f"feed{k}"))
        core.feed(j)
        return c

    lax.fori_loop(0, core.chunks, feed, 0)
    last = units * (core.steps - 1)
    for h in (0, 1):
        core.fetch_probs(last, h).start()
    tick("fed")
    core.norm_two_back()
    put_result = pltpu.make_async_copy(r["second"], result, r["in_sem"].at[0])
    put_result.start()
    tick("normed")
    core.output_back()
    for s in range(core.steps - 1, -1, -1):
        if s == 0:
            fetch_qkv.wait()
        each_unit(f"back{s}.", functools.partial(core.attend_back, s))
        if s == 2:
            core.normed_back(s)
            core.project_back(s)
            fetch_qkv = pltpu.make_async_copy(qkv_hbm, r["qkv"].at[0], r["in_sem"].at[2])
            fetch_qkv.start()
            put_result.wait()
            fetch_x = pltpu.make_async_copy(x, r["second"], r["in_sem"].at[0])
            fetch_x.start()
        else:
            core.normed_back(s)
            core.project_back(s)
        tick(f"back{s}")
    fetch_x.wait()
    tick("last")
    core.norm_one_back()
    put_gtok = pltpu.make_async_copy(r["n2"], gtok, r["in_sem"].at[1])
    put_gtok.start()
    tick("end")
    put_gtok.wait()


def linked_plan():
    plan = {}

    def add(name, *events):
        plan.setdefault(name, []).extend(events)

    def g(stage, *groups):
        return [("gather", k, stage) for k in groups]

    add("start", *[("own", k, 0) for k in range(12)], *g(0, 0, 1), ("small", 0, 0), *g(0, *range(2, 12)))
    add("start", *g(1, 0, 1))
    add("head", ("small", 0, 1), *g(2, 0, 1), ("small", 0, 2), *g(1, 2, 3), ("small", 0, 3), ("small", 0, 4))
    add("project0", *g(3, 0, 1), *g(4, 0))
    add("attend0.0", *g(2, 2, 3))
    add("attend0.1", *g(1, 4, 5))
    add("attend0.3", *g(3, 2, 3))
    add("project1", *g(4, 1))
    add("attend1.0", *g(4, 2, 3), *g(2, 4, 5))
    add("attend1.1", *g(1, 6, 7))
    add("attend1.3", *g(3, 4, 5))
    add("attend2.0", *g(4, 4, 5), *g(2, 6, 7))
    add("attend2.1", *g(1, 8, 9))
    add("attend2.3", *g(3, 6, 7))
    add("output", *g(4, 6, 7), *g(2, 8, 9), *g(1, 10, 11))
    add("feed0", *g(3, 8, 9), *g(4, 8, 9), *g(2, 10, 11))
    add("feed1", *g(3, 10, 11))
    add("feed2", *g(4, 10, 11))
    ticks = ["feed1", "feed2", "feed3", "fed", "normed"]
    ticks += ["back2.0", "back2.1", "back2.2", "back2.3", "back2", "back1.1", "back1.2", "back1.3", "back1", "back0.1", "back0.2", "back0.3", "back0"]
    entry = ["feed1", "feed2", "feed3", "fed", "fed", "normed", "normed", "back2.0", "back2.0", "back2", "back1", "back0"]
    for i, name in enumerate(ticks):
        for stage in range(4, -1, -1):
            for p in range(12):
                if ticks.index(entry[p]) + stage == i:
                    add(name, ("scatter", p, stage))
    add("last", ("scatter", 11, 1))
    add("end", ("small", 1, 0), ("scatter", 11, 2), ("small", 1, 1), ("scatter", 11, 3), ("small", 1, 2), ("small", 1, 3), ("scatter", 11, 4), ("small", 1, 4))
    return plan


GROUPS = [("wqkv", 0), ("wqkv", 1), ("wqkv", 2), ("wo", 0), ("down", 0), ("up", 0), ("down", 1), ("down", 2), ("down", 3), ("up", 1), ("up", 2), ("up", 3)]
SUMMED = [5, 9, 10, 11, 4, 6, 7, 8, 3, 2, 1, 0]


def linked_kernel(length, names, x, cot, onehot, bias, placed, qw, kw, vw, ow, uw, dw, result, gtok, gpack, small, e_hbm, qkv_hbm, *scratch):
    r = dict(zip(names, scratch), onehot=onehot, bias=bias, small=small)
    width = r["mix"].shape[1]
    cut, half, steps = width // 16, width // 2, r["wqkv"].shape[0]
    f = lax.axis_index("fsdp")

    def view(kind, k):
        if kind == "wo":
            return r["wo"]
        if kind == "down":
            return r["down"].at[:, :, :, pl.ds(cut * k, cut)]
        return r[kind].at[k]

    def sources(kind, k):
        if kind == "wo":
            return [(ow, 0, half)]
        if kind == "down":
            return [(dw.at[pl.ds(cut * k, cut)], 0, half)]
        if kind == "up":
            at = pl.multiple_of((k + f * (1 - 2 * (k % 2))) * half, 128)
            return [(uw.at[:, pl.ds(at, half)], 0, half)]
        return [(w.at[:, pl.ds(128 * k, 128)], 128 * i, 128) for i, w in enumerate((qw, kw, vw))]

    links = Links(r, [view(*g) for g in GROUPS], [sources(*g) for g in GROUPS], gpack)
    plan = linked_plan()
    act = dict(own=lambda g, stage: links.own(g), gather=links.gather, scatter=links.scatter, small=links.small_sum)

    def tick(name, ask=False):
        if ask:
            return bool(plan.get(name))
        for kind, index, stage in plan.get(name, ()):
            act[kind](index, stage)

    r["vec"][...] = placed[...]
    links.greet()
    layer(length, r, dict(x=x, cot=cot, result=result, gtok=gtok, e_hbm=e_hbm, qkv_hbm=qkv_hbm), tick, True)


def end_kernel(result, gtok, gpack, small, result_out, gtok_out, gq, gk, gv, go, gu, gd, gvec, gub, sem):
    copies = [pltpu.make_async_copy(result, result_out, sem.at[0]), pltpu.make_async_copy(gtok, gtok_out, sem.at[1])]
    for copy in copies:
        copy.start()
    dp, f = lax.axis_index("dp"), lax.axis_index("fsdp")
    cut, half = gpack.shape[1:]
    for g, (kind, k) in enumerate(GROUPS):
        block = gpack[g]
        if kind == "wo":
            go[...] = block
        elif kind == "down":
            gd[cut * k : cut * k + cut, :] = block
        elif kind == "up":
            gu[:, pl.ds(pl.multiple_of((k + f * (1 - 2 * (k % 2))) * half, 128), half)] = block
        else:
            for i, out in enumerate((gq, gk, gv)):
                out[:, 128 * k : 128 * k + 128] = block[:, 128 * i : 128 * i + 128]
    width = small.shape[1]
    rows, lanes = gvec.shape
    vec = pltpu.roll(small[...], lax.rem(width - lanes * dp, width), 1)[:, :128]
    gvec[...] = jnp.where(f == 0, vec[:rows], vec[rows : 2 * rows])[:, :lanes]
    row, at = bias_place(dp, f, gub.shape[1], half)
    line = pltpu.roll(small[...], lax.rem(width - at, width), 1)[:, :128]
    picked = lax.broadcasted_iota(jnp.int32, line.shape, 0) == row
    gub[...] = jnp.sum(jnp.where(picked, line, 0.0), axis=0, keepdims=True)[:, : gub.shape[1]]
    for copy in copies:
        copy.wait()


def bias_place(dp, f, size, half):
    first = (dp * 2 + f) * size
    unit, inside = first // half, first % half
    chunk = unit % 4
    second = unit // 4
    chunk = chunk + second * (1 - 2 * (chunk % 2))
    return 8 + chunk, second * half + inside


def linked(tokens, groups, step_valid, qw, kw, vw, ow, uw, dw, vectors, up_bias, cotangent):
    items, length, width = tokens.shape
    rows, ff = items * length, up_bias.shape[0] * 32
    dp, f = lax.axis_index("dp"), lax.axis_index("fsdp")
    onehot, bias = masks(groups, step_valid)
    placed = jnp.zeros((16, width), f32)
    placed = lax.dynamic_update_slice(placed, vectors.astype(f32), (f * vectors.shape[0], dp * vectors.shape[1]))
    placed = lax.dynamic_update_slice(placed, up_bias.astype(f32)[None], bias_place(dp, f, up_bias.shape[0], width // 2))
    cut, half, count = width // 16, width // 2, len(GROUPS)
    S = jax.ShapeDtypeStruct
    scratch = dict(local_scratch(rows, length, width, ff), **link_scratch(count, cut, width, 2))
    vm, hb = pl.BlockSpec(memory_space=VMEM), pl.BlockSpec(memory_space=pl.ANY)
    pairs = width // 64
    result, gtok, gpack, small, _, _ = pl.pallas_call(
        functools.partial(linked_kernel, length, list(scratch)),
        out_shape=(
            S((rows, width), bf),
            S((rows, width), bf),
            S((count, cut, half), f32),
            S((16, width), f32),
            S((items * pairs, length, length), bf),
            S((rows, width), bf),
        ),
        in_specs=[hb, hb, vm, vm, vm] + [hb] * 6,
        out_specs=(hb, hb, vm, vm, hb, hb),
        scratch_shapes=list(scratch.values()),
        compiler_params=pltpu.CompilerParams(vmem_limit_bytes=64 << 20, collective_id=1, has_side_effects=True),
    )(tokens.reshape(rows, width), cotangent.reshape(rows, width), onehot, bias, placed, qw, kw, vw, ow, uw, dw)
    shapes = [S((rows, width), bf)] * 2 + [S(w.shape, f32) for w in (qw, kw, vw, ow, uw, dw, vectors)] + [S((1,) + up_bias.shape, f32)]
    outs = pl.pallas_call(
        end_kernel,
        out_shape=tuple(shapes),
        in_specs=[vm, vm, vm, vm],
        out_specs=(hb, hb) + (vm,) * 8,
        scratch_shapes=[DMA((2,))],
    )(result, gtok, gpack, small)
    return (outs[0].reshape(tokens.shape), outs[1].reshape(tokens.shape), *outs[2:9], outs[9].reshape(up_bias.shape))


def local_kernel(length, names, x, cot, onehot, bias, vec, wqkv, wo, up, down, result, gtok, small, gqkv, go, gup, gdown, e_hbm, qkv_hbm, *scratch):
    r = dict(zip(names, scratch), onehot=onehot, bias=bias, small=small, vec=vec)
    pairs = zip((wqkv, wo, up, down), (gqkv, go, gup, gdown), WEIGHTS)
    pairs = [(into, out, r[name], r["w_sem"].at[i]) for i, (into, out, name) in enumerate(pairs)]

    def tick(name, ask=False):
        if ask:
            return False
        for into, out, mine, sem in pairs:
            if name == "start":
                pltpu.make_async_copy(into, mine, sem).start()
            if name == "head":
                pltpu.make_async_copy(into, mine, sem).wait()
            if name == "end":
                pltpu.make_async_copy(mine, out, sem).start()
        if name == "end":
            for into, out, mine, sem in pairs:
                pltpu.make_async_copy(mine, out, sem).wait()

    layer(length, r, dict(x=x, cot=cot, result=result, gtok=gtok, e_hbm=e_hbm, qkv_hbm=qkv_hbm), tick, False)


def chunk_units(chunks):
    return [(j, chunks + (j ^ 1)) for j in range(chunks)]


def local(tokens, groups, step_valid, weights, vectors, up_bias, cotangent):
    qw, kw, vw, ow, uw, dw = weights
    items, length, width = tokens.shape
    rows, ff = items * length, up_bias.shape[0]
    steps, half, chunks = width // 256, width // 2, ff // width
    scratch = dict(local_scratch(rows, length, width, ff), w_sem=DMA((4,)))
    parts = [[w[:, 128 * p : 128 * p + 128] for w in (qw, kw, vw)] for p in range(2 * steps)]
    wqkv = jnp.stack([jnp.concatenate(parts[s] + parts[s + steps], axis=1) for s in range(steps)])
    units = chunk_units(chunks)
    up = jnp.stack([jnp.concatenate([uw[:, half * k : half * k + half] for k in two], axis=1) for two in units])
    lines = [jnp.concatenate([up_bias[half * k : half * k + half] for k in two]) for two in units]
    vec = jnp.concatenate([vectors, jnp.stack(lines), jnp.zeros((8 - chunks, width), bf)]).astype(f32)
    whole = [w.reshape(scratch[name].shape) for w, name in zip((wqkv, ow, up, dw), WEIGHTS)]
    S = jax.ShapeDtypeStruct
    vm, hb = pl.BlockSpec(memory_space=VMEM), pl.BlockSpec(memory_space=pl.ANY)
    result, gtok, small, gqkv, go, gup, gdown, _, _ = pl.pallas_call(
        functools.partial(local_kernel, length, list(scratch)),
        out_shape=(
            S((rows, width), bf),
            S((rows, width), bf),
            S((16, width), f32),
            *[S(w.shape, bf) for w in whole],
            S((items * width // 64, length, length), bf),
            S((rows, width), bf),
        ),
        in_specs=[hb, hb, vm, vm, vm] + [hb] * 4,
        out_specs=(hb, hb, vm) + (hb,) * 6,
        scratch_shapes=list(scratch.values()),
        compiler_params=pltpu.CompilerParams(vmem_limit_bytes=64 << 20),
    )(tokens.reshape(rows, width), cotangent.reshape(rows, width), *masks(groups, step_valid), vec, *whole)
    gqkv, gup = gqkv.reshape(steps, width, width), gup.reshape(chunks, width, width)
    grads = []
    for w in range(3):
        at = [(p % steps, (p // steps) * 384 + 128 * w) for p in range(2 * steps)]
        grads.append(jnp.concatenate([gqkv[s][:, k : k + 128] for s, k in at], axis=1))
    place = {k: (j, i) for j, two in enumerate(units) for i, k in enumerate(two)}
    order = [place[k] for k in range(2 * chunks)]
    gup = jnp.concatenate([gup[j][:, half * i : half * i + half] for j, i in order], axis=1)
    gub = jnp.concatenate([small[8 + j, half * i : half * i + half] for j, i in order])
    grads += [go.reshape(ow.shape), gup, gdown.reshape(dw.shape)]
    return result.reshape(tokens.shape), gtok.reshape(tokens.shape), grads, small[:8], gub


def gathered(tokens, groups, step_valid, qw, kw, vw, ow, uw, dw, vectors, up_bias, cotangent):
    def whole(w):
        return lax.all_gather(lax.all_gather(w, "fsdp", axis=1, tiled=True), "dp", axis=0, tiled=True)

    def shard(g):
        return lax.psum_scatter(lax.psum_scatter(g, "dp", scatter_dimension=0, tiled=True), "fsdp", scatter_dimension=1, tiled=True)

    vec = lax.all_gather(lax.all_gather(vectors, "fsdp", axis=0, tiled=True), "dp", axis=1, tiled=True)
    line = lax.all_gather(up_bias, ("dp", "fsdp"), axis=0, tiled=True)
    weights = [whole(w) for w in (qw, kw, vw, ow, uw, dw)]
    result, gtok, grads, gvec, gub = local(tokens, groups, step_valid, weights, vec, line, cotangent)
    gvec = lax.psum_scatter(lax.psum_scatter(gvec, "dp", scatter_dimension=1, tiled=True), "fsdp", scatter_dimension=0, tiled=True)
    gub = lax.psum_scatter(gub, ("dp", "fsdp"), scatter_dimension=0, tiled=True)
    return (result, gtok, *[shard(g.astype(f32)) for g in grads], gvec, gub)


def solution(mesh):
    linked_mesh = mesh.shape["dp"] == 16 and mesh.shape["fsdp"] == 2
    items, both = P(("dp", "fsdp"), None, None), P("dp", "fsdp")
    pairs, line = P(("dp", "fsdp"), None), P(("dp", "fsdp"))
    return jax.shard_map(
        linked if linked_mesh else gathered,
        mesh=mesh,
        in_specs=(items, pairs, pairs) + (both,) * 6 + (P("fsdp", "dp"), line, items),
        out_specs=(items, items) + (both,) * 6 + (P("fsdp", "dp"), line),
        check_vma=False,
    )
```

```python
import functools

import jax
import jax.numpy as jnp
from jax import lax
from jax.experimental import pallas as pl
from jax.experimental.pallas import tpu as pltpu
from jax.sharding import PartitionSpec as P

bf = jnp.bfloat16
f32 = jnp.float32
NN = (((1,), (0,)), ((), ()))
NT = (((1,), (1,)), ((), ()))
TN = (((0,), (0,)), ((), ()))
HD = 64
EPS = 1e-6
MESH = pl.DeviceIdType.MESH
VMEM = pltpu.VMEM
DMA = pltpu.SemaphoreType.DMA


def dg(a, b, dims):
    return lax.dot_general(a, b, dims, preferred_element_type=f32)


def mat(ref):
    block = ref[...]
    return block.reshape(-1, block.shape[-1])


def normalized(x):
    center = x - jnp.mean(x, axis=-1, keepdims=True)
    r = lax.rsqrt(jnp.mean(center * center, axis=-1, keepdims=True) + EPS)
    return center * r, r


def fold8(x):
    return jnp.sum(x.reshape(-1, 8, x.shape[-1]), axis=0)


def each_block(rows, body, sums=None, size=32, together=5):
    step = size * together
    whole = rows // step

    def several(blocks):
        parts = [body(at, n) for at, n in blocks]
        for i in range(len(parts[0] or ())):
            sums[i] += sum(part[i] for part in parts)

    def one(i, c):
        several([(pl.ds(pl.multiple_of(i * step + k * size, 16), size), size) for k in range(together)])
        return c

    lax.fori_loop(0, whole, one, 0)
    if whole * step < rows:
        several([(pl.ds(at, min(size, rows - at)), min(size, rows - at)) for at in range(whole * step, rows, size)])


class Core:
    def __init__(self, rows, length, width, chunks, refs):
        self.rows, self.length, self.width, self.chunks = rows, length, width, chunks
        self.items = rows // length
        self.pairs = width // 128
        self.steps = self.pairs // 2
        self.__dict__.update(refs)

    def blocks(self):
        half = (self.length // 2 + 15) // 16 * 16
        return ((0, half), (half, self.length - half))

    def norm_one(self):
        def block(at, size):
            self.res[at, :] = normalized(self.x[at, :].astype(f32))[0]

        each_block(self.rows, block)

    def norm_one_scaled(self):
        gain, shift = self.vec[0:1, :], self.vec[1:2, :]

        def block(at, size):
            self.normed[at, :] = (self.res[at, :] * gain + shift).astype(bf)

        each_block(self.rows, block)

    def project(self, s):
        step = self.steps

        def three(p):
            at = slice(128 * p, 128 * p + 128)
            return [self.vec[2:3, at], jnp.zeros((1, 128), f32), self.vec[3:4, at]]

        bias = jnp.concatenate(three(s) + three(s + step), axis=1)
        lane = lax.broadcasted_iota(jnp.int32, (1, self.width), 1) % 384
        scale = jnp.where(lane < 128, HD**-0.5, 1.0).astype(f32)
        out = (dg(self.normed[...], mat(self.wqkv.at[s]), NN) + bias) * scale
        self.qkv[s % 2] = out.astype(bf)

    def place(self, s, u):
        item, half = u // 2, u % 2
        rows = pl.ds(pl.multiple_of(item * self.length, 16), self.length)
        cols = [pl.ds(pl.multiple_of(half * 384 + 128 * w, 128), 128) for w in range(3)]
        wide = pl.ds(pl.multiple_of((s + half * self.steps) * 128, 128), 128)
        return rows, cols, wide

    def low(self):
        return lax.broadcasted_iota(jnp.int32, (self.length, 128), 1) < HD

    def attend(self, s, u):
        n = 2 * self.items
        rows, cols, wide = self.place(s, u)
        q, k, v = [self.qkv[s % 2, rows, at] for at in cols]
        g, b = self.onehot[rows, :], self.bias[rows, :]
        low = self.low()
        t = s * n + u
        slot = lax.rem(t, 2)

        @pl.when(t >= 2)
        def _():
            for h in (0, 1):
                self.keep_probs(t - 2, h).wait()

        outs = []
        for h in (0, 1):
            mine = low if h == 0 else ~low
            qa, ka = jnp.where(mine, q, g), jnp.where(mine, k, b)
            va = jnp.where(mine, v, jnp.ones_like(v))
            parts = []
            for at, size in self.blocks():
                scores = dg(qa[at : at + size], ka, NT)
                e = jnp.exp(scores - jnp.max(scores, axis=1, keepdims=True)).astype(bf)
                self.ebuf[slot, h, at : at + size, :] = e
                parts.append(dg(e, va, NN))
            outs.append(jnp.concatenate(parts, axis=0))
        total = pltpu.roll(jnp.where(low, outs[1], outs[0]), HD, 1)
        inv = 1.0 / total
        self.linv[rows, wide] = inv.astype(bf)
        self.mix[rows, wide] = (jnp.where(low, outs[0], outs[1]) * inv).astype(bf)
        for h in (0, 1):
            self.keep_probs(t, h).start()

    def keep_probs(self, t, h):
        return pltpu.make_async_copy(self.ebuf.at[lax.rem(t, 2), h], self.e_hbm.at[2 * t + h], self.e_sem.at[lax.rem(t, 2), h])

    def attend_end(self):
        last = 2 * self.items * self.steps
        for t in (last - 2, last - 1):
            for h in (0, 1):
                self.keep_probs(t, h).wait()

    def output(self):
        self.res[...] = dg(self.mix[...], mat(self.wo), NN)
        shift0, gain, shift = self.vec[4:5, :], self.vec[5:6, :], self.vec[6:7, :]

        def block(at, size):
            middle = self.res[at, :] + self.x[at, :].astype(f32) + shift0
            self.res[at, :] = middle
            n, r = normalized(middle)
            self.n2[at, :] = n.astype(bf)
            self.r2[at, :] = jnp.broadcast_to(r, (size, 128))
            self.second[at, :] = (n * gain + shift).astype(bf)

        each_block(self.rows, block)
        self.gsec[...] = jnp.zeros_like(self.gsec)

    def feed(self, j, between):
        z, y = lax.div(j, 2), lax.rem(j, 2)
        first, other = self.down.at[z, y], self.down.at[2 + z, 1 - y]
        up = mat(self.up.at[j])
        down = jnp.concatenate([mat(first), mat(other)], axis=0)
        bias = self.vec[pl.ds(8 + j, 1), :]
        c0, c1 = 0.7978845608028654, 0.7978845608028654 * 0.044715

        def item(i, c):
            pl.when(i == 1)(functools.partial(between, ".3"))
            for at, size in self.blocks():
                rows = pl.ds(pl.multiple_of(i * self.length + at, 16), size)
                u = dg(self.second[rows, :], up, NN) + bias
                gh = dg(self.cot[rows, :], down, NT)
                u2 = u * u
                s = 0.5 + 0.5 * jnp.tanh(u * (c0 + c1 * u2))
                hid = u * s
                slope = s + (hid * (1.0 - s)) * (2 * c0 + (6 * c1) * u2)
                gp = gh * slope
                hid, gp = hid.astype(bf), gp.astype(bf)
                self.hid[rows, :] = hid
                self.gp[rows, :] = gp
                self.sums8[1] += fold8(gp.astype(f32))
                self.res[rows, :] += dg(hid, down, NN)
                self.gsec[rows, :] += dg(gp, up, NT)
            return c

        self.sums8[1] = jnp.zeros_like(self.sums8[1])
        lax.fori_loop(0, self.items, item, 0)
        self.small[pl.ds(12 + j, 1), :] = jnp.sum(self.sums8[1], axis=0, keepdims=True)
        between(".5")
        gup = dg(self.second[...], self.gp[...], TN).astype(bf)
        self.up[j] = gup.reshape(self.up.shape[1:])
        gdown = dg(self.hid[...], self.cot[...], TN).astype(bf)
        half = gdown.shape[0] // 2
        first[...] = gdown[:half].reshape(first.shape)
        other[...] = gdown[half:].reshape(other.shape)

    def norm_two_back(self):
        gain, last = self.vec[5:6, :], self.vec[7:8, :]
        self.sums8[...] = jnp.zeros_like(self.sums8)

        def block(at, size):
            self.result[at, :] = (self.res[at, :] + last).astype(bf)
            gs, n, r = self.gsec[at, :], self.n2[at, :].astype(f32), self.r2[at, 0:1]
            ct = self.cot[at, :].astype(f32)
            e = gs * gain
            gm = ct + r * (e - jnp.mean(e, axis=-1, keepdims=True) - n * jnp.mean(e * n, axis=-1, keepdims=True))
            gb = gm.astype(bf)
            self.gsec[at, :] = gm
            self.gp[at, :] = gb
            return fold8(gb.astype(f32)), fold8(gs * n), fold8(gs), fold8(ct)

        each_block(self.rows, block, self.sums8)
        for i in range(4):
            self.small[8 + i : 9 + i, :] = jnp.sum(self.sums8[i], axis=0, keepdims=True)

    def output_back(self):
        self.hid[...] = dg(self.gp[...], mat(self.wo), NT).astype(bf)
        self.wo[...] = dg(self.mix[...], self.gp[...], TN).astype(bf).reshape(self.wo.shape)

    def fetch_probs(self, t, h):
        return pltpu.make_async_copy(self.e_hbm.at[2 * t + h], self.ebuf.at[lax.rem(t, 2), h], self.e_sem.at[lax.rem(t, 2), h])

    def attend_back(self, s, u):
        n = 2 * self.items
        rows, cols, wide = self.place(s, u)
        t = s * n + u
        after = t + 1 - lax.div(u + 1, n) * 2 * n
        slot = lax.rem(t, 2)

        @pl.when(after >= 0)
        def _():
            for h in (0, 1):
                self.fetch_probs(after, h).start()

        q, k, v = [self.qkv[s % 2, rows, at] for at in cols]
        low = self.low()
        lane = lax.broadcasted_iota(jnp.int32, (self.length, 128), 1) % HD
        across = lax.broadcasted_iota(jnp.int32, (128, 128), 0) // HD != lax.broadcasted_iota(jnp.int32, (128, 128), 1) // HD
        across = jnp.where(across, 1.0, 0.0).astype(bf)
        go = self.hid[rows, wide].astype(f32) * self.linv[rows, wide].astype(f32)
        gob = go.astype(bf)
        inner = dg((go * self.mix[rows, wide].astype(f32)).astype(bf), across, NN)
        high = inner.astype(bf)
        rest = (inner - high.astype(f32)).astype(bf)
        minus = jnp.where(lane == 0, -high, jnp.where(lane == 1, -rest, jnp.zeros_like(high)))
        for h in (0, 1):
            self.fetch_probs(t, h).wait()
        qt, kt, gt = q.T, k.T, gob.T
        dq, dk, dv = [], [], []
        for h in (0, 1):
            mine = low if h == 0 else ~low
            ga, va = jnp.where(mine, gob, minus), jnp.where(mine, v, jnp.ones_like(v))
            at_h = slice(HD * h, HD * h + HD)
            for at, size in self.blocks():
                gprobs = dg(ga[at : at + size], va, NT)
                self.dsbuf[at : at + size, :] = (self.ebuf[slot, h, at : at + size, :].astype(f32) * gprobs).astype(bf)
            ds, e = self.dsbuf[...], self.ebuf[slot, h]
            dq.append(dg(kt[at_h], ds, NT))
            dk.append(dg(qt[at_h], ds, NN))
            dv.append(dg(gt[at_h], e, NN))
        parts = []
        for at, part, scale in zip(cols, (dq, dk, dv), (HD**-0.5, 1.0, 1.0)):
            whole = (jnp.concatenate(part, axis=0) * scale).T
            low_part = whole.astype(bf)
            self.gps[s][rows, at] = low_part
            parts.append(jnp.sum(low_part.astype(f32), axis=0, keepdims=True))
        self.small[2:3, wide] += parts[0]
        self.small[3:4, wide] += parts[2]

    def project_back(self, s):
        into = self.up.at[self.steps - 1 - s]
        into[...] = dg(self.normed[...], self.gps[s][...], TN).astype(bf).reshape(into.shape)

    def normed_back(self, s):
        part = dg(self.gps[s][...], mat(self.wqkv.at[s]), NT)
        if s == self.steps - 1:
            self.res[...] = part
        else:
            self.res[...] += part

    def norm_one_sums(self):
        self.sums8[...] = jnp.zeros_like(self.sums8)

        def block(at, size):
            n, _ = normalized(self.x_back[at, :].astype(f32))
            gn = self.res[at, :]
            return fold8(gn * n), fold8(gn)

        each_block(self.rows, block, self.sums8)
        for i in range(2):
            self.small[i : i + 1, :] = jnp.sum(self.sums8[i], axis=0, keepdims=True)

    def norm_one_back(self):
        gain = self.vec[0:1, :]

        def block(at, size):
            n, r = normalized(self.x_back[at, :].astype(f32))
            e = self.res[at, :] * gain
            gt = self.gsec[at, :] + r * (e - jnp.mean(e, axis=-1, keepdims=True) - n * jnp.mean(e * n, axis=-1, keepdims=True))
            self.gtok[at, :] = gt.astype(bf)

        each_block(self.rows, block)

    def masks(self):
        steps = self.step_valid.shape[1]
        group = lax.broadcasted_iota(jnp.int32, (128, self.length), 0) % HD
        for i in range(self.items):
            rows = slice(i * self.length, (i + 1) * self.length)
            key = self.groups[i : i + 1, :]
            alive = jnp.where(key == 0, 1.0, 0.0)
            for t in range(steps):
                valid = (self.step_valid[i, t] == 1).astype(f32)
                alive += jnp.where((key == 2 * t + 1) | (key == 2 * t + 2), 1.0, 0.0) * valid
            linked = (key == 0) | (key == group) | ((key % 2 == 1) & (key < group))
            seen = jnp.where(linked, 1.0, 0.0) * alive
            hidden = jnp.where(group <= 2 * steps, (1.0 - seen) * -1e30, 0.0)
            self.onehot[rows, :] = jnp.where(key == group, 1.0, 0.0).astype(bf).T
            self.bias[rows, :] = hidden.astype(bf).T

def sum_parts(p, rows):
    if p == len(SUMMED) - 1:
        third = rows // 3
        return [(i * third, third, order) for i, order in enumerate(("xyz", "yxz", "zyx"))]
    return [(0, rows, SUM_ORDERS[p])]


def got_name(p, order, stage):
    p = p - 8 if 8 <= p <= 10 else p
    return f"got_{p}_{order}_{stage}"


class Links:
    def __init__(self, refs, views, back_views, sources, sums):
        dp = lax.axis_index("dp")
        self.f = lax.axis_index("fsdp")
        self.z, self.y, self.c = dp // 4, (dp // 2) % 2, dp % 2
        self.views, self.back_views, self.sources, self.sums = views, back_views, sources, sums
        self.numbers = {}
        self.__dict__.update(refs)

    def at(self, z=None, y=None, c=None, f=None):
        z = self.z if z is None else z
        y = self.y if y is None else y
        c = self.c if c is None else c
        f = self.f if f is None else f
        return (z * 4 + y * 2 + c, f)

    def along_z(self, d):
        return self.at(z=(self.z + d) % 4)

    def across(self, axis):
        return dict(x=self.at(f=1 - self.f), y=self.at(y=1 - self.y), c=self.at(c=1 - self.c))[axis]

    def greet(self):
        barrier = pltpu.get_barrier_semaphore()
        for peer in [self.along_z(d) for d in (1, 2, 3)] + [self.across(axis) for axis in "xyc"]:
            pl.semaphore_signal(barrier, inc=1, device_id=peer, device_id_type=MESH)
        pl.semaphore_wait(barrier, 6)

    def half(self, f, width):
        return pl.ds(pl.multiple_of(f * (width // 2), 128), width // 2)

    def send(self, src, dst, name, peer):
        sem = self.numbers.setdefault(name, len(self.numbers))
        return pltpu.make_async_remote_copy(
            src_ref=src,
            dst_ref=dst,
            send_sem=self.send_sem.at[sem],
            recv_sem=self.recv_sem.at[sem],
            device_id=peer,
            device_id_type=MESH,
        )

    def own_copies(self, g):
        view = self.views[g]
        first = self.f * (view.shape[-1] // 2)
        copies = []
        for i, (piece, at, size) in enumerate(self.sources[g]):
            spot = view.at[self.z, self.y, self.c, :, pl.ds(pl.multiple_of(first + at, 128), size)]
            copies.append(pltpu.make_async_copy(piece, spot, self.own_sem.at[3 * g + i]))
        return copies

    def own(self, g):
        for copy in self.own_copies(g):
            copy.start()

    def gather_parts(self, g):
        rows = self.views[g].shape[3]
        if g == 0:
            third = rows // 3
            return [(i * third, third, order) for i, order in enumerate(("zxy", "zyx", "xyz"))]
        return [(0, rows, ORDERS[g])]

    def gather_copies(self, g, stage):
        view = self.views[g]
        if stage == 3:
            part = view.at[:, :, self.c]
            return [self.send(part, part, ("gather", g, 3), self.across("c"))]
        copies = []
        for first, size, order in self.gather_parts(g):
            done, axis = order[:stage], order[stage]
            z = slice(None) if "z" in done else self.z
            y = slice(None) if "y" in done else self.y
            columns = slice(None) if "x" in done else self.half(self.f, view.shape[-1])
            part = view.at[z, y, self.c, pl.ds(first, size), columns]
            peers = [self.along_z(d) for d in (1, 2, 3)] if axis == "z" else [self.across(axis)]
            copies += [self.send(part, part, ("gather", g, order, axis, i), peer) for i, peer in enumerate(peers)]
        return copies

    def gather(self, g, stage):
        for copy in self.own_copies(g) if stage == 0 else self.gather_copies(g, stage - 1):
            copy.wait()
        if stage < 4:
            for copy in self.gather_copies(g, stage):
                copy.start()

    def scatter_copies(self, p, stage):
        view = self.back_views[p]
        if stage == 0:
            return [self.send(view.at[:, :, 1 - self.c], self.got_c.at[p % self.got_c.shape[0]], ("scatter", p), self.across("c"))]
        copies = []
        for first, size, order in sum_parts(p, view.shape[3]):
            done, axis = order[: stage - 1], order[stage - 1]
            got = getattr(self, got_name(p, order, stage))
            steps = (1, 2, 3) if axis == "z" else (1,)
            for i, d in enumerate(steps):
                z = (self.z + d) % 4 if axis == "z" else self.z if "z" in done else slice(None)
                y = 1 - self.y if axis == "y" else self.y if "y" in done else slice(None)
                columns = slice(None)
                if axis == "x" or "x" in done:
                    columns = self.half(1 - self.f if axis == "x" else self.f, view.shape[-1])
                part = view.at[z, y, self.c, pl.ds(first, size), columns]
                peer = self.along_z(d) if axis == "z" else self.across(axis)
                copies.append(self.send(part, got.at[i], ("scatter", p, order, axis, i), peer))
        return copies

    def put_sum(self, p):
        slot = p % self.stage.shape[0]
        return pltpu.make_async_copy(self.stage.at[slot], self.sums.at[SUMMED[p]], self.put_sem.at[slot])

    def scatter(self, p, stage):
        view = self.back_views[p]
        slots = self.got_c.shape[0]
        if stage > 0:
            for copy in self.scatter_copies(p, stage - 1):
                copy.wait()
        if stage == 4 and p >= self.stage.shape[0]:
            self.put_sum(p - self.stage.shape[0]).wait()
        if stage == 1:
            for z in range(4):
                for y in range(2):
                    view[z, y, self.c] += self.got_c[p % slots, z, y]
            if p + slots < len(self.views):
                pl.semaphore_signal(self.free_sem, inc=1, device_id=self.across("c"), device_id_type=MESH)
        if stage > 1:
            for first, size, order in sum_parts(p, view.shape[3]):
                done = order[: stage - 1]
                got = getattr(self, got_name(p, order, stage - 1))
                rows = pl.ds(first, size)
                columns = self.half(self.f, view.shape[-1]) if "x" in done else slice(None)
                if stage == 4:
                    total = view[self.z, self.y, self.c, rows, columns].astype(f32)
                    for i in range(got.shape[0]):
                        total += got[i].astype(f32)
                    self.stage[p % self.stage.shape[0], rows, :] = total
                    continue
                for z in (self.z,) if "z" in done else range(4):
                    for y in (self.y,) if "y" in done else range(2):
                        spot = (() if "z" in done else (z,)) + (() if "y" in done else (y,))
                        view[z, y, self.c, rows, columns] += sum(got[(i,) + spot] for i in range(got.shape[0]))
        if stage == 0 and p >= slots:
            pl.semaphore_wait(self.free_sem, 1)
        if stage == 4:
            self.put_sum(p).start()
            if p == len(SUMMED) - 1:
                for last in range(p + 1 - self.stage.shape[0], p + 1):
                    self.put_sum(last).wait()
        if stage < 4:
            for copy in self.scatter_copies(p, stage):
                copy.start()

    def small_copies(self, which, stage):
        mine = (self.vec_low, self.small.at[0:8], self.small.at[8:16])[which]
        got = self.got_vec if which == 0 else self.got_small.at[which - 1]
        if stage == 0:
            return [self.send(mine, got.at[d - 1], ("small", which, 0, d), self.along_z(d)) for d in (1, 2, 3)]
        return [self.send(mine, got.at[2 + stage], ("small", which, stage), self.across("xyc"[stage - 1]))]

    def small_sum(self, which, stage):
        mine = (self.vec_low, self.small.at[0:8], self.small.at[8:16])[which]
        got = self.got_vec if which == 0 else self.got_small.at[which - 1]
        if stage > 0:
            for copy in self.small_copies(which, stage - 1):
                copy.wait()
            mine[...] += got[0] + got[1] + got[2] if stage == 1 else got[1 + stage]
        if stage < 4:
            for copy in self.small_copies(which, stage):
                copy.start()
        elif which == 0:
            self.vec[...] = self.vec_low[...].astype(f32)

    def place_vec(self, vectors, up_bias):
        rows, lanes = vectors.shape
        width = self.small.shape[1]
        row, at = bias_place(lax.axis_index("dp"), self.f, up_bias.shape[1], width // 2)
        self.small[...] = jnp.zeros_like(self.small)
        part = vectors[...].astype(f32)
        self.small[0:rows, 0:lanes] = part
        self.small[rows : 2 * rows, 0:lanes] = part
        self.small[8:9, 0 : up_bias.shape[1]] = up_bias[...].astype(f32)
        both = self.small[...]
        line = jnp.broadcast_to(both[8:9], both.shape)
        place = lax.broadcasted_iota(jnp.int32, both.shape, 0)
        vec = jnp.where((place < 2 * rows) & (place // rows == self.f), pltpu.roll(both, lanes * lax.axis_index("dp"), 1), 0.0)
        self.vec_low[...] = (vec + jnp.where(place == 8 + row, pltpu.roll(line, at, 1), 0.0)).astype(bf)


def link_scratch(groups, rows, width, slots):
    got = {}
    for p in range(groups):
        for _, size, order in sum_parts(p, rows):
            for stage in (1, 2, 3):
                done = order[:stage]
                shape = (3 if order[stage - 1] == "z" else 1,)
                shape += (() if "z" in done else (4,)) + (() if "y" in done else (2,))
                got[got_name(p, order, stage)] = VMEM(shape + (size, width // 2 if "x" in done else width), bf)
    return dict(
        vec=VMEM((16, width), f32),
        vec_low=VMEM((16, width), bf),
        got_vec=VMEM((6, 16, width), bf),
        got_small=VMEM((2, 6, 8, width), f32),
        got_c=VMEM((slots, 4, 2, rows, width), bf),
        **got,
        stage=VMEM((3, rows, width // 2), f32),
        put_sem=DMA((3,)),
        send_sem=DMA((16 * groups,)),
        recv_sem=DMA((16 * groups,)),
        own_sem=DMA((3 * groups,)),
        free_sem=pltpu.SemaphoreType.REGULAR,
    )


WEIGHTS = ("wqkv", "wo", "up", "down")


def local_scratch(rows, length, width, ff):
    whole = (rows, width)
    steps, cut = width // 256, width // 16
    return dict(
        wqkv=VMEM((steps, 4, 2, 2, cut, width), bf),
        wo=VMEM((4, 2, 2, cut, width), bf),
        up=VMEM((ff // width, 4, 2, 2, cut, width), bf),
        down=VMEM((4, 2, 2, ff // 16, width), bf),
        cot=VMEM(whole, bf),
        normed=VMEM(whole, bf),
        qkv=VMEM((2,) + whole, bf),
        mix=VMEM(whole, bf),
        linv=VMEM(whole, bf),
        res=VMEM(whole, f32),
        n2=VMEM(whole, bf),
        r2=VMEM((rows, 128), f32),
        second=VMEM(whole, bf),
        gsec=VMEM(whole, f32),
        hid=VMEM(whole, bf),
        gp=VMEM(whole, bf),
        ebuf=VMEM((2, 2, length, length), bf),
        dsbuf=VMEM((length, length), bf),
        sums8=VMEM((4, 8, width), f32),
        onehot=VMEM((rows, 128), bf),
        bias=VMEM((rows, 128), bf),
        e_sem=DMA((2, 2)),
        in_sem=DMA((4,)),
    )


def layer(length, core_refs, hbm, tick, links_on):
    r = core_refs
    rows, width = r["mix"].shape
    x, cot, result, gtok, qkv_hbm = [hbm[k] for k in ("x", "cot", "result", "gtok", "qkv_hbm")]
    steps = r["wqkv"].shape[0]
    gps = [r["qkv"].at[1], r["n2"], r["gp"]]
    staged = dict(x=r["hid"], x_back=r["second"], result=r["second"], gtok=r["hid"], gps=gps, e_hbm=hbm["e_hbm"])
    core = Core(rows, length, width, r["up"].shape[0], dict(r, **staged))
    load_x = pltpu.make_async_copy(x, r["hid"], r["in_sem"].at[0])
    load_cot = pltpu.make_async_copy(cot, r["cot"], r["in_sem"].at[1])
    keep_qkv = pltpu.make_async_copy(r["qkv"].at[0], qkv_hbm, r["in_sem"].at[2])
    units = 2 * core.items

    def each_unit(name, work):
        def one(u, c):
            for k in range(units):
                if tick(name + str(k), True):
                    pl.when(u == k)(functools.partial(tick, name + str(k)))
            work(u)
            return c

        lax.fori_loop(0, units, one, 0)

    load_x.start()
    load_cot.start()
    tick("start")
    r["small"][...] = jnp.zeros_like(r["small"])
    load_x.wait()
    core.norm_one()
    tick("head")
    core.masks()
    tick("vec")
    core.norm_one_scaled()
    for s in range(core.steps):
        tick(f"project{s}")
        if s == 2:
            keep_qkv.wait()
        core.project(s)
        if s == 0:
            keep_qkv.start()
        each_unit(f"attend{s}.", functools.partial(core.attend, s))
    core.attend_end()
    tick("output")
    core.output()
    load_cot.wait()

    def feed(j, c):
        def point(end):
            for k in range(core.chunks):
                name = f"feed{k}{end}"
                if tick(name, True):
                    pl.when(j == k)(functools.partial(tick, name))

        point("")
        core.feed(j, point)
        return c

    lax.fori_loop(0, core.chunks, feed, 0)
    last = units * (core.steps - 1)
    for h in (0, 1):
        core.fetch_probs(last, h).start()
    tick("fed")
    core.norm_two_back()
    put_result = pltpu.make_async_copy(r["second"], result, r["in_sem"].at[0])
    put_result.start()
    tick("normed")
    core.output_back()
    for s in range(core.steps - 1, -1, -1):
        if s == 0:
            fetch_qkv.wait()
        each_unit(f"back{s}.", functools.partial(core.attend_back, s))
        core.project_back(s)
        if s == steps - 1:
            fetch_qkv = pltpu.make_async_copy(qkv_hbm, r["qkv"].at[0], r["in_sem"].at[2])
            fetch_qkv.start()
            put_result.wait()
            fetch_x = pltpu.make_async_copy(x, r["second"], r["in_sem"].at[0])
            fetch_x.start()
        tick(f"back{s}")
    for s in range(steps - 1, -1, -1):
        core.normed_back(s)
        tick(f"left{s}")
    fetch_x.wait()
    core.norm_one_sums()
    tick("sums")
    core.norm_one_back()
    put_gtok = pltpu.make_async_copy(r["hid"], gtok, r["in_sem"].at[1])
    put_gtok.start()
    tick("end")
    put_gtok.wait()


def linked_plan():
    plan = {}

    def add(name, *events):
        plan.setdefault(name, []).extend(events)

    def g(stage, *groups):
        return [("gather", k, stage) for k in groups]

    add("start", *[("own", k, 0) for k in range(12)], ("vec", 0, 0), *g(0, 0, 1), ("small", 0, 1), *g(1, 0))
    add("head", ("small", 0, 2), *g(2, 0), *g(0, 2, 3, 4, 5, 6, 8, 9, 7), *g(1, 1))
    add("vec", ("small", 0, 3), ("small", 0, 4))
    add("project0", *g(3, 0), *g(4, 0), *g(2, 1))
    add("attend0.0", *g(1, 2, 7))
    add("attend0.2", *g(1, 3), *g(2, 2))
    add("attend0.3", *g(3, 1), *g(1, 4))
    add("project1", *g(4, 1))
    add("attend1.0", *g(2, 7))
    add("attend1.1", *g(2, 3), *g(1, 6, 5))
    add("attend1.2", *g(2, 4))
    add("attend1.3", *g(1, 8), *g(0, 10, 11), *g(3, 2))
    add("project2", *g(4, 2))
    add("attend2.0", *g(3, 3), *g(2, 6))
    add("attend2.1", *g(2, 8), *g(4, 3))
    add("attend2.2", *g(2, 5))
    add("attend2.3", *g(3, 7), *g(1, 9))
    add("output", *g(3, 4, 6), *g(4, 7))
    add("feed0", *g(4, 4, 6), *g(1, 10), *g(3, 8, 5), *g(4, 8, 5))
    add("feed0.3", *g(2, 9))
    add("feed0.5", *g(2, 10), *g(1, 11))
    add("feed1", *g(3, 9), *g(4, 9))
    add("feed1.3", *g(2, 11))
    add("feed1.5", *g(3, 10))
    add("feed2", *g(4, 10))
    add("feed2.3", *g(3, 11))
    add("feed2.5", *g(4, 11))
    for p, points in enumerate(SUM_POINTS):
        for stage, name in enumerate(points):
            add(name, ("scatter", p, stage))
    add("back2.1", ("small", 2, 0))
    add("back2.3", ("small", 2, 1))
    add("back1.1", ("small", 2, 2))
    add("back1.2", ("small", 2, 3))
    add("back1.3", ("small", 2, 4))
    add("sums", ("small", 1, 0))
    add("end", ("small", 1, 1), ("scatter", 11, 3), ("small", 1, 2), ("scatter", 9, 4))
    add("end", ("small", 1, 3), ("scatter", 10, 4), ("small", 1, 4), ("scatter", 11, 4))
    for name, events in plan.items():
        if name == "end":
            continue
        events.sort(key=lambda e: -e[2] if e[0] == "scatter" else 0)
    return plan


GROUPS = [("wqkv", 0), ("wqkv", 1), ("wqkv", 2), ("wo", 0), ("down", 0), ("up", 0), ("down", 1), ("down", 2), ("down", 3), ("up", 1), ("up", 2), ("up", 3)]
ORDERS = [None, "zxy", "zxy", "zyx", "zxy", "zyx", "zyx", "xyz", "zxy", "zxy", "zyx", "zxy"]
SUMMED = [5, 9, 10, 11, 4, 6, 7, 8, 3, 2, 1, 0]
SUM_ORDERS = ["xyz", "yxz", "xyz", "yxz", "xyz", "yxz", "xyz", "yxz", "xyz", "yxz", "xyz"]
SUM_POINTS = [
    ("feed1", "feed1.3", "feed2", "feed2.3", "feed2.5"),
    ("feed2", "feed2.3", "feed3", "feed3.3", "feed3.5"),
    ("feed3", "feed3.3", "fed", "normed", "back2.1"),
    ("fed", "normed", "back2.2", "back1.2", "back1"),
    ("fed", "normed", "back2.2", "back1.2", "back1"),
    ("normed", "back2.0", "back1.0", "back1", "back0.2"),
    ("normed", "back2.0", "back1.0", "back1", "back0"),
    ("back2.1", "back1.0", "back0.2", "back0", "left1"),
    ("back2.2", "back1.0", "back0.2", "back0", "left1"),
    ("back1.0", "back1.2", "back0", "left0"),
    ("back1", "back0.0", "back0", "left0"),
    ("back0", "left2", "sums"),
]


def linked_kernel(length, names, x, cot, groups, step_valid, vectors, up_bias, qw, kw, vw, ow, uw, dw, result, gtok, gpack, small, e_hbm, qkv_hbm, *scratch):
    r = dict(zip(names, scratch), groups=groups, step_valid=step_valid, small=small)
    width = r["mix"].shape[1]
    cut, half, steps = width // 16, width // 2, r["wqkv"].shape[0]
    f = lax.axis_index("fsdp")

    def view(kind, k):
        if kind == "wo":
            return r["wo"]
        if kind == "down":
            return r["down"].at[:, :, :, pl.ds(cut * k, cut)]
        return r[kind].at[k]

    def sources(kind, k):
        if kind == "wo":
            return [(ow, 0, half)]
        if kind == "down":
            return [(dw.at[pl.ds(cut * k, cut)], 0, half)]
        if kind == "up":
            at = pl.multiple_of((k + f * (1 - 2 * (k % 2))) * half, 128)
            return [(uw.at[:, pl.ds(at, half)], 0, half)]
        return [(w.at[:, pl.ds(128 * k, 128)], 128 * i, 128) for i, w in enumerate((qw, kw, vw))]

    back_views = [view("up", steps - 1 - k) if kind == "wqkv" else view(kind, k) for kind, k in (GROUPS[g] for g in SUMMED)]
    links = Links(r, [view(*g) for g in GROUPS], back_views, [sources(*g) for g in GROUPS], gpack)
    plan = linked_plan()

    def vec(which, stage):
        links.place_vec(vectors, up_bias)
        links.small_sum(which, stage)

    act = dict(own=lambda g, stage: links.own(g), vec=vec, gather=links.gather, scatter=links.scatter, small=links.small_sum)

    def tick(name, ask=False):
        if ask:
            return bool(plan.get(name))
        for kind, index, stage in plan.get(name, ()):
            act[kind](index, stage)

    links.greet()
    layer(length, r, dict(x=x, cot=cot, result=result, gtok=gtok, e_hbm=e_hbm, qkv_hbm=qkv_hbm), tick, True)


def end_kernel(result, gtok, gpack, small, result_out, gtok_out, gq, gk, gv, go, gu, gd, gvec, gub, sem):
    copies = [pltpu.make_async_copy(result, result_out, sem.at[0]), pltpu.make_async_copy(gtok, gtok_out, sem.at[1])]
    for copy in copies:
        copy.start()
    dp, f = lax.axis_index("dp"), lax.axis_index("fsdp")
    cut, half = gpack.shape[1:]
    for g, (kind, k) in enumerate(GROUPS):
        block = gpack[g]
        if kind == "wo":
            go[...] = block
        elif kind == "down":
            gd[cut * k : cut * k + cut, :] = block
        elif kind == "up":
            gu[:, pl.ds(pl.multiple_of((k + f * (1 - 2 * (k % 2))) * half, 128), half)] = block
        else:
            for i, out in enumerate((gq, gk, gv)):
                out[:, 128 * k : 128 * k + 128] = block[:, 128 * i : 128 * i + 128]
    width = small.shape[1]
    rows, lanes = gvec.shape
    vec = pltpu.roll(small[...], lax.rem(width - lanes * dp, width), 1)[:, :128]
    gvec[...] = jnp.where(f == 0, vec[:rows], vec[8 : 8 + rows])[:, :lanes]
    row, at = bias_place(dp, f, gub.shape[1], half)
    line = pltpu.roll(small[...], lax.rem(width - at, width), 1)[:, :128]
    picked = lax.broadcasted_iota(jnp.int32, line.shape, 0) == 12 + row
    gub[...] = jnp.sum(jnp.where(picked, line, 0.0), axis=0, keepdims=True)[:, : gub.shape[1]]
    for copy in copies:
        copy.wait()


def bias_place(dp, f, size, half):
    first = (dp * 2 + f) * size
    unit, inside = first // half, first % half
    chunk = unit % 4
    second = unit // 4
    chunk = chunk + second * (1 - 2 * (chunk % 2))
    return chunk, second * half + inside


def linked(tokens, groups, step_valid, qw, kw, vw, ow, uw, dw, vectors, up_bias, cotangent):
    items, length, width = tokens.shape
    rows, ff = items * length, up_bias.shape[0] * 32
    cut, half, count = width // 16, width // 2, len(GROUPS)
    S = jax.ShapeDtypeStruct
    scratch = dict(local_scratch(rows, length, width, ff), **link_scratch(count, cut, width, 2))
    vm, hb = pl.BlockSpec(memory_space=VMEM), pl.BlockSpec(memory_space=pl.ANY)
    pairs = width // 64
    result, gtok, gpack, small, _, _ = pl.pallas_call(
        functools.partial(linked_kernel, length, list(scratch)),
        out_shape=(
            S((rows, width), bf),
            S((rows, width), bf),
            S((count, cut, half), f32),
            S((16, width), f32),
            S((items * pairs, length, length), bf),
            S((rows, width), bf),
        ),
        in_specs=[hb, hb, vm, pl.BlockSpec(memory_space=pltpu.SMEM), vm, vm] + [hb] * 6,
        out_specs=(hb, hb, hb, vm, hb, hb),
        scratch_shapes=list(scratch.values()),
        compiler_params=pltpu.CompilerParams(vmem_limit_bytes=64 << 20, collective_id=1, has_side_effects=True),
    )(tokens.reshape(rows, width), cotangent.reshape(rows, width), groups, step_valid, vectors, up_bias[None], qw, kw, vw, ow, uw, dw)
    shapes = [S((rows, width), bf)] * 2 + [S(w.shape, f32) for w in (qw, kw, vw, ow, uw, dw, vectors)] + [S((1,) + up_bias.shape, f32)]
    outs = pl.pallas_call(
        end_kernel,
        out_shape=tuple(shapes),
        in_specs=[vm, vm, vm, vm],
        out_specs=(hb, hb) + (vm,) * 8,
        scratch_shapes=[DMA((2,))],
    )(result, gtok, gpack, small)
    return (outs[0].reshape(tokens.shape), outs[1].reshape(tokens.shape), *outs[2:9], outs[9].reshape(up_bias.shape))


def local_kernel(length, names, x, cot, groups, step_valid, vec, wqkv, wo, up, down, result, gtok, small, gqkv, go, gup, gdown, e_hbm, qkv_hbm, *scratch):
    r = dict(zip(names, scratch), groups=groups, step_valid=step_valid, small=small, vec=vec)
    pairs = zip((wqkv, wo, up, down), (gqkv, go, gup, gdown), WEIGHTS)
    pairs = [(into, out, r[name], r["w_sem"].at[i]) for i, (into, out, name) in enumerate(pairs)]

    def tick(name, ask=False):
        if ask:
            return False
        steps = gqkv.shape[0]
        done = []
        if name == "fed":
            done = [pltpu.make_async_copy(r["up"], gup, r["w_sem"].at[2])]
        if name == "end":
            done = [pltpu.make_async_copy(r["up"].at[steps - 1 - s], gqkv.at[s], r["w_sem"].at[s]) for s in range(steps)]
            done += [pltpu.make_async_copy(r["wo"], go, r["w_sem"].at[3]), pltpu.make_async_copy(r["down"], gdown, r["w_sem"].at[4])]
        for into, out, mine, sem in pairs:
            if name == "start":
                pltpu.make_async_copy(into, mine, sem).start()
            if name == "head":
                pltpu.make_async_copy(into, mine, sem).wait()
        for copy in done:
            copy.start()
        for copy in done:
            copy.wait()

    layer(length, r, dict(x=x, cot=cot, result=result, gtok=gtok, e_hbm=e_hbm, qkv_hbm=qkv_hbm), tick, False)


def chunk_units(chunks):
    return [(j, chunks + (j ^ 1)) for j in range(chunks)]


def local(tokens, groups, step_valid, weights, vectors, up_bias, cotangent):
    qw, kw, vw, ow, uw, dw = weights
    items, length, width = tokens.shape
    rows, ff = items * length, up_bias.shape[0]
    steps, half, chunks = width // 256, width // 2, ff // width
    scratch = dict(local_scratch(rows, length, width, ff), w_sem=DMA((5,)))
    parts = [[w[:, 128 * p : 128 * p + 128] for w in (qw, kw, vw)] for p in range(2 * steps)]
    wqkv = jnp.stack([jnp.concatenate(parts[s] + parts[s + steps], axis=1) for s in range(steps)])
    units = chunk_units(chunks)
    up = jnp.stack([jnp.concatenate([uw[:, half * k : half * k + half] for k in two], axis=1) for two in units])
    lines = [jnp.concatenate([up_bias[half * k : half * k + half] for k in two]) for two in units]
    vec = jnp.concatenate([vectors, jnp.stack(lines), jnp.zeros((8 - chunks, width), bf)]).astype(f32)
    whole = [w.reshape(scratch[name].shape) for w, name in zip((wqkv, ow, up, dw), WEIGHTS)]
    S = jax.ShapeDtypeStruct
    vm, hb = pl.BlockSpec(memory_space=VMEM), pl.BlockSpec(memory_space=pl.ANY)
    result, gtok, small, gqkv, go, gup, gdown, _, _ = pl.pallas_call(
        functools.partial(local_kernel, length, list(scratch)),
        out_shape=(
            S((rows, width), bf),
            S((rows, width), bf),
            S((16, width), f32),
            *[S(w.shape, bf) for w in whole],
            S((items * width // 64, length, length), bf),
            S((rows, width), bf),
        ),
        in_specs=[hb, hb, vm, pl.BlockSpec(memory_space=pltpu.SMEM), vm] + [hb] * 4,
        out_specs=(hb, hb, vm) + (hb,) * 6,
        scratch_shapes=list(scratch.values()),
        compiler_params=pltpu.CompilerParams(vmem_limit_bytes=64 << 20),
    )(tokens.reshape(rows, width), cotangent.reshape(rows, width), groups, step_valid, vec, *whole)
    gqkv, gup = gqkv.reshape(steps, width, width), gup.reshape(chunks, width, width)
    grads = []
    for w in range(3):
        at = [(p % steps, (p // steps) * 384 + 128 * w) for p in range(2 * steps)]
        grads.append(jnp.concatenate([gqkv[s][:, k : k + 128] for s, k in at], axis=1))
    place = {k: (j, i) for j, two in enumerate(units) for i, k in enumerate(two)}
    order = [place[k] for k in range(2 * chunks)]
    gup = jnp.concatenate([gup[j][:, half * i : half * i + half] for j, i in order], axis=1)
    gub = jnp.concatenate([small[12 + j, half * i : half * i + half] for j, i in order])
    grads += [go.reshape(ow.shape), gup, gdown.reshape(dw.shape)]
    gvec = jnp.concatenate([small[:4], small[8:12]])
    return result.reshape(tokens.shape), gtok.reshape(tokens.shape), grads, gvec, gub


def gathered(tokens, groups, step_valid, qw, kw, vw, ow, uw, dw, vectors, up_bias, cotangent):
    def whole(w):
        return lax.all_gather(lax.all_gather(w, "fsdp", axis=1, tiled=True), "dp", axis=0, tiled=True)

    def shard(g):
        return lax.psum_scatter(lax.psum_scatter(g, "dp", scatter_dimension=0, tiled=True), "fsdp", scatter_dimension=1, tiled=True)

    vec = lax.all_gather(lax.all_gather(vectors, "fsdp", axis=0, tiled=True), "dp", axis=1, tiled=True)
    line = lax.all_gather(up_bias, ("dp", "fsdp"), axis=0, tiled=True)
    weights = [whole(w) for w in (qw, kw, vw, ow, uw, dw)]
    result, gtok, grads, gvec, gub = local(tokens, groups, step_valid, weights, vec, line, cotangent)
    gvec = lax.psum_scatter(lax.psum_scatter(gvec, "dp", scatter_dimension=1, tiled=True), "fsdp", scatter_dimension=0, tiled=True)
    gub = lax.psum_scatter(gub, ("dp", "fsdp"), scatter_dimension=0, tiled=True)
    return (result, gtok, *[shard(g.astype(f32)) for g in grads], gvec, gub)


def solution(mesh):
    linked_mesh = mesh.shape["dp"] == 16 and mesh.shape["fsdp"] == 2
    items, both = P(("dp", "fsdp"), None, None), P("dp", "fsdp")
    pairs, line = P(("dp", "fsdp"), None), P(("dp", "fsdp"))
    return jax.shard_map(
        linked if linked_mesh else gathered,
        mesh=mesh,
        in_specs=(items, pairs, pairs) + (both,) * 6 + (P("fsdp", "dp"), line, items),
        out_specs=(items, items) + (both,) * 6 + (P("fsdp", "dp"), line),
        check_vma=False,
    )
```
